512 devices in a mesh: tm: 16 (over y, x), seq: 32 (over z, core).
Axes of the slice: x: 4, y: 4, z: 16, core: 2. Of those that a mesh axis runs over, the one named last changes fastest.
Arguments:
- latent_start: float32 [2048, 64], P('seq'), may hold values from -6 to 6
- noise: float32 [16, 2048, 64], P('tm', 'seq'), may hold values from -6 to 6
- step_index: int32 [16], P('tm'), may hold values from 0 to 49
- camera_ids: int32 [2048], P('seq'), may hold values from 0 to 5
- embed_in: bfloat16 [64, 2048], replicated, may hold values from -0.75 to 0.75
- time_table: float32 [50, 2048], replicated, may hold values from -6 to 6
- camera_table: float32 [6, 2048], replicated, may hold values from -6 to 6
- norm_gain: float32 [2048], replicated, may hold values from 0.25 to 1.75
- qkv_weight: bfloat16 [2048, 32, 192], P(None, 'seq'), as said below
- final_gain: float32 [2048], replicated, may hold values from 0.25 to 1.75
- out_weight: bfloat16 [2048, 64], replicated, may hold values from -0.125 to 0.125
- step_sizes: float32 [50], replicated, may hold values from 0.1 to 0.4
- noise_scales: float32 [50], replicated, may hold values from 0.1 to 0.4
Outputs:
- latents_out: float32 [16, 2048, 64], P('tm', 'seq')
The draws below stay inside these ranges and needn't reach their ends.
Inputs may be any that keep to these rules, and one draw needn't show every extreme that they name: `qkv_weight`: every entry lies within 26 / sqrt(2048) in magnitude.
All inputs are finite; a program needn't handle non-finite values.
Results may differ from the reference program's by a relative error of at most 0.002.
Values may be sent and summed in bfloat16 or wider, within the bound.
A program may use at most 64 MiB of HBM per device.

```python
import math
import jax
import jax.numpy as jnp
from jax import lax

D = 2048
HSIZE = 64
C = 64
CAMS = 6
NSTEP = 50
TOKENS = 2048
HEADS = 32
WINDOW = 16


def draw_qkv_weight(key, part):
    key = jax.random.fold_in(key, 7)
    base_key, head_key, power_key = jax.random.split(key, 3)
    base = jax.random.truncated_normal(base_key, -3.0, 3.0, (D, HEADS, 3 * HSIZE), jnp.float32)
    aligned_count = 2
    power_lo = 28.0
    power_hi = 60.0
    order = jax.random.permutation(head_key, HEADS)
    chosen = jnp.zeros((HEADS,), jnp.float32).at[order[:aligned_count]].set(1.0)
    power = jnp.exp(jax.random.uniform(power_key, (HEADS,), jnp.float32, math.log(power_lo), math.log(power_hi)))
    factor = 1.0 + chosen * (jnp.sqrt(power) - 1.0)
    query = base[:, :, :HSIZE] * factor[None, :, None]
    other_keys = base[:, :, HSIZE:2 * HSIZE]
    keys = chosen[None, :, None] * query + (1.0 - chosen[None, :, None]) * other_keys
    values = base[:, :, 2 * HSIZE:]
    joined = jnp.concatenate([query, keys, values], axis=2) * D ** (-0.5)
    return joined.astype(jnp.bfloat16)


def plant(entries, own_key, smallest, largest):
    index_at = [jax.random.randint(jax.random.fold_in(own_key, axis), (), 0, length) for axis, length in enumerate(entries.shape)]
    widest = entries.shape.index(max(entries.shape))
    neighbour = index_at[:widest] + [(index_at[widest] + 1) % entries.shape[widest]] + index_at[widest + 1:]
    return entries.at[tuple(index_at)].set(smallest).at[tuple(neighbour)].set(largest)


def shard_levels(rng, dims, shards, low, top_value):
    def one(axis_at, blocks):
        heights = jax.random.uniform(jax.random.fold_in(jax.random.fold_in(rng, 6), axis_at), (blocks,), jnp.float32, low / len(shards), top_value / len(shards))
        return jnp.repeat(jnp.exp(heights), dims[axis_at] // blocks).reshape((-1,) + (1,) * (len(dims) - axis_at - 1))

    factor_of = one(*shards[0])
    for cut in shards[1:]:
        factor_of = factor_of * one(*cut)
    return factor_of


def gaussian(stream_key, extent, deviation, bound, cuts=(), kind=jnp.bfloat16):
    factor_of = shard_levels(stream_key, extent, cuts, -0.22, 0.18) if cuts else 1.0
    drawn = jax.random.normal(stream_key, extent, jnp.float32) * deviation * factor_of
    return jnp.minimum(jnp.maximum(drawn, -bound), bound).astype(kind)


def setup_inputs(seed: int = 0) -> dict:
    key_of = jax.random.split(jax.random.key(seed), 14)
    return {
        "latent_start": gaussian(key_of[0], (TOKENS, C), 1.0, 6.0, ((0, 32),), jnp.float32),
        "noise": gaussian(key_of[1], (WINDOW, TOKENS, C), 1.0, 6.0, ((0, 16), (1, 32)), jnp.float32),
        "step_index": plant(jax.random.randint(key_of[2], (WINDOW,), 0, NSTEP), jax.random.fold_in(key_of[2], 1), 0, NSTEP - 1).astype(jnp.int32),
        "camera_ids": plant(jax.random.randint(key_of[3], (TOKENS,), 0, CAMS), jax.random.fold_in(key_of[3], 1), 0, CAMS - 1).astype(jnp.int32),
        "embed_in": gaussian(key_of[4], (C, D), C ** -0.5, 0.75),
        "time_table": gaussian(key_of[5], (NSTEP, D), 1.0, 6.0, (), jnp.float32),
        "camera_table": gaussian(key_of[6], (CAMS, D), 1.0, 6.0, (), jnp.float32),
        "norm_gain": jnp.clip(1.0 + 0.15 * jax.random.normal(key_of[7], (D,), jnp.float32), 0.25, 1.75),
        "qkv_weight": draw_qkv_weight(jax.random.fold_in(key_of[13], 71), 0),
        "final_gain": jnp.clip(1.0 + 0.15 * jax.random.normal(key_of[9], (D,), jnp.float32), 0.25, 1.75),
        "out_weight": gaussian(key_of[10], (D, C), D ** -0.5, 0.125),
        "step_sizes": jnp.clip(jnp.exp(jax.random.uniform(key_of[11], (NSTEP,), jnp.float32, math.log(0.1), math.log(0.4))), 0.1, 0.4),
        "noise_scales": jnp.clip(jnp.exp(jax.random.uniform(key_of[12], (NSTEP,), jnp.float32, math.log(0.1), math.log(0.4))), 0.1, 0.4),
    }


def rms_scale(value, gain):
    return value * lax.rsqrt(lax.optimization_barrier(jnp.mean(value * value, axis=-1, keepdims=True)) + 1e-06) * gain

def attend(qkv):
    total = qkv.shape[0]
    hsize = qkv.shape[1] // 3
    query = qkv[:, :hsize]
    keys = qkv[:, hsize:2 * hsize]
    values = qkv[:, 2 * hsize:]
    block = 512 if total % 512 == 0 else total
    blocks = query.reshape(total // block, block, hsize)

    def one_block(rows):
        scores = jnp.dot(rows, keys.T, preferred_element_type=jnp.float32) * hsize ** (-0.5)
        peak = lax.optimization_barrier(jnp.max(scores, axis=-1, keepdims=True))
        expo = jnp.exp(scores - peak)
        probs = (expo / lax.optimization_barrier(jnp.sum(expo, axis=-1, keepdims=True))).astype(jnp.bfloat16)
        return jnp.dot(probs, values, preferred_element_type=jnp.float32).astype(jnp.bfloat16)
    return lax.map(one_block, blocks).reshape(total, hsize)

def drift_of(latent, tau, camera_rows, embed_in, time_table, norm_gain, qkv_weight, final_gain, out_weight):
    hidden = jnp.dot(latent.astype(jnp.bfloat16), embed_in, preferred_element_type=jnp.float32)
    hidden = hidden + time_table[tau][None, :] + camera_rows
    normed = rms_scale(hidden, norm_gain).astype(jnp.bfloat16)

    def one_head(weight):
        qkv = jnp.dot(normed, weight, preferred_element_type=jnp.float32).astype(jnp.bfloat16)
        return attend(qkv)
    heads_out = lax.map(one_head, jnp.moveaxis(qkv_weight, 1, 0))
    joined = jnp.moveaxis(heads_out, 0, 1).reshape(hidden.shape[0], -1)
    mixed = rms_scale(hidden + joined.astype(jnp.float32), final_gain).astype(jnp.bfloat16)
    return jnp.dot(mixed, out_weight, preferred_element_type=jnp.float32)

def reference(latent_start, noise, step_index, camera_ids, embed_in, time_table, camera_table, norm_gain, qkv_weight, final_gain, out_weight, step_sizes, noise_scales):
    window = noise.shape[0]
    camera_rows = camera_table[camera_ids]
    latents = [latent_start for step in range(window)]
    inclusive = None
    for sweep in range(2):
        terms = []
        for step in range(window):
            tau = step_index[step]
            drift = drift_of(latents[step], tau, camera_rows, embed_in, time_table, norm_gain, qkv_weight, final_gain, out_weight)
            terms.append(step_sizes[tau] * drift + noise_scales[tau] * noise[step])
        stacked = jnp.stack(terms)
        inclusive = jnp.cumsum(stacked, axis=0)
        exclusive = jnp.concatenate([jnp.zeros_like(stacked[:1]), inclusive[:-1]], axis=0)
        latents = [latent_start + exclusive[step] for step in range(window)]
    return latent_start[None] + inclusive
```

```python
import functools
import math

import jax
import jax.numpy as jnp
from jax import lax
from jax.experimental import pallas as pl
from jax.experimental.pallas import tpu as pltpu
from jax.sharding import PartitionSpec as P

MESH = pl.DeviceIdType.MESH
F32 = jnp.float32
BF16 = jnp.bfloat16
TOK = 64
HALF = 32
CHIPS = 16
STEPS = 16
BLOCK = 512
RELAYS = ((9, 16), (3, 9), (0, 3))


def slot_offset(slot):
    half = slot // 2
    return 8 + half - (slot % 2) * (1 + 2 * half)


def mirror(slot):
    return 0 if slot == 0 else 15 if slot == 15 else slot + 1 if slot % 2 else slot - 1


def dot(a, b):
    return jnp.dot(a, b, preferred_element_type=F32)


def dot_nt(a, b):
    return lax.dot_general(a, b, (((1,), (1,)), ((), ())), preferred_element_type=F32)


def split2(value):
    high = value.astype(BF16)
    return high, (value - high.astype(F32)).astype(BF16)


def split3(value):
    high = value.astype(BF16)
    rest = value - high.astype(F32)
    middle = rest.astype(BF16)
    return high, middle, (rest - middle.astype(F32)).astype(BF16)


def pack(block):
    flipped = block.T
    return jnp.concatenate([flipped[:HALF], flipped[HALF:]], axis=1)


def kernel(
    ls_ref, noise_ref, step_ref, cam_ref, embed_ref, time_ref, camt_ref, ngain_ref, w_ref,
    fgain_ref, wout_ref, sizes_ref, scales_ref,
    out_ref,
    lsp, noisep, gb0, gb1, u, mw, hw, gw, table, ncol, wot, fgt, k2, vt, qt, ht, s0, s1,
    pout, pin, term, prefix,
    gsend, grecv, rsend, rrecv, msend, mrecv, psend, precv, tsend, trecv,
):
    tm, sq = lax.axis_index("tm"), lax.axis_index("seq")
    z, c = sq // 2, sq % 2
    other = 1 - c
    partner = (tm, 2 * z + other)

    def along(offset):
        return (tm, 2 * ((z + offset) % CHIPS) + c)

    barrier = pltpu.get_barrier_semaphore()

    def greet_z(i, carry):
        pl.semaphore_signal(barrier, inc=1, device_id=along(i), device_id_type=MESH)
        return carry

    def greet_tm(i, carry):
        pl.semaphore_signal(
            barrier, inc=1, device_id=((tm + i) % STEPS, sq), device_id_type=MESH
        )
        return carry

    lax.fori_loop(1, CHIPS, greet_z, 0)
    lax.fori_loop(1, STEPS, greet_tm, 0)
    pl.semaphore_signal(barrier, inc=1, device_id=partner, device_id_type=MESH)

    lsp[...] = pack(ls_ref[...])
    gb0[c, 15, 0:HALF, :] = lsp[...].astype(BF16)
    cam = cam_ref[...].astype(F32).astype(BF16)
    gb0[c, 15, HALF:48, :] = jnp.broadcast_to(jnp.concatenate([cam, cam], axis=1), (16, 128))

    pl.semaphore_wait(barrier, CHIPS - 1 + STEPS - 1 + 1)

    def gather_copy(buf, phase, slot):
        return pltpu.make_async_remote_copy(
            src_ref=buf.at[c, 15],
            dst_ref=buf.at[c, mirror(slot)],
            send_sem=gsend.at[phase, slot],
            recv_sem=grecv.at[phase, mirror(slot)],
            device_id=along(slot_offset(slot)),
            device_id_type=MESH,
        )

    def gather_wait(buf, phase, slot):
        return pltpu.make_async_remote_copy(
            src_ref=buf.at[c, 15],
            dst_ref=buf.at[c, slot],
            send_sem=gsend.at[phase, slot],
            recv_sem=grecv.at[phase, slot],
            device_id=along(slot_offset(slot)),
            device_id_type=MESH,
        )

    def relay_copy(buf, phase, index, core):
        first, last = RELAYS[index]
        part = buf.at[core, pl.ds(first, last - first)]
        return pltpu.make_async_remote_copy(
            src_ref=part,
            dst_ref=part,
            send_sem=rsend.at[phase, index],
            recv_sem=rrecv.at[phase, index],
            device_id=partner,
            device_id_type=MESH,
        )

    def gather_start(buf, phase):
        for slot in range(15):
            gather_copy(buf, phase, slot).start()

    def gather_finish(buf, phase):
        for index, (first, last) in enumerate(RELAYS):
            for slot in reversed(range(first, min(last, 15))):
                gather_wait(buf, phase, slot).wait_recv()
            relay_copy(buf, phase, index, c).start()
        for index in range(len(RELAYS)):
            relay_copy(buf, phase, index, other).wait_recv()
        for slot in range(15):
            gather_copy(buf, phase, slot).wait_send()
        for index in range(len(RELAYS)):
            relay_copy(buf, phase, index, c).wait_send()

    def assemble(buf, cameras):
        for side in range(2):
            core = c if side == 0 else other
            for pair in range(8):
                lanes = slice(side * 1024 + pair * 128, side * 1024 + pair * 128 + 128)
                left = buf[core, 2 * pair]
                right = buf[core, 2 * pair + 1]
                low = jnp.concatenate([left[:, :64], right[:, :64]], axis=1)
                high = jnp.concatenate([left[:, 64:], right[:, 64:]], axis=1)
                tile = jnp.concatenate([low[:HALF], high[:HALF]], axis=0)
                u[0:64, lanes] = tile
                u[64:128, lanes] = tile
                u[128:192, lanes] = tile
                if cameras:
                    ids = low[HALF : HALF + 16].astype(F32)
                    row = lax.broadcasted_iota(jnp.int32, (16, 128), 0).astype(F32)
                    one = jnp.where(ids == row, 1.0, 0.0).astype(BF16)
                    u[192:208, lanes] = one
                    u[208:224, lanes] = one
                    u[224:240, lanes] = one

    gather_start(gb0, 0)

    tau = step_ref[0]
    rows = camt_ref[...] + time_ref[pl.ds(tau, 1), :]
    rows = jnp.concatenate([rows, jnp.zeros((10, rows.shape[1]), F32)], axis=0)
    table[...] = rows
    embed = embed_ref[...]
    gain = ngain_ref[...]
    eg_high, eg_low = split2(embed.astype(F32) * gain)
    rg_high, rg_low = split2(rows * gain)
    folded = dot(jnp.concatenate([eg_high, rg_high, eg_low, rg_low], axis=0), w_ref[...])
    fold_x = folded[0:64] + folded[80:144]
    fold_e = folded[64:80] + folded[144:160]
    fx_high = fold_x.astype(BF16).astype(F32)
    fe_high = fold_e.astype(BF16).astype(F32)
    width = fold_x.shape[1]
    stacked = jnp.concatenate(
        [
            fx_high, fold_x - fx_high, jnp.zeros((64, width), F32),
            fe_high, fold_e - fe_high, jnp.zeros((32, width), F32),
        ],
        axis=0,
    )
    mw[c] = stacked.T.astype(BF16)
    exchange = pltpu.make_async_remote_copy(
        src_ref=mw.at[c], dst_ref=mw.at[c], send_sem=msend, recv_sem=mrecv,
        device_id=partner, device_id_type=MESH,
    )
    exchange.start()

    gram = dot_nt(embed, embed)
    r_high, r_middle, r_low = split3(rows)
    cross = 2.0 * (dot_nt(r_low, embed) + dot_nt(r_middle, embed) + dot_nt(r_high, embed))
    g3 = [part.astype(F32) for part in split3(gram)]
    c3 = [part.astype(F32) for part in split3(cross)]
    gw[...] = jnp.concatenate(g3 + c3 + [jnp.zeros((16, 64), F32)], axis=0).T.astype(BF16)
    ncol[...] = jnp.broadcast_to(jnp.sum(rows * rows, axis=1, keepdims=True), ncol.shape)

    columns = pl.ds(pl.multiple_of(z * 128, 128), 128)
    h3 = [part.astype(F32) for part in split3(table[:, columns])]
    hw[...] = jnp.concatenate(
        [embed_ref[:, columns].astype(F32), jnp.zeros((128, 128), F32)]
        + h3
        + [jnp.zeros((16, 128), F32)],
        axis=0,
    ).T.astype(BF16)
    fgt[...] = jnp.broadcast_to(fgain_ref[:, columns], (128, 128)).T
    wot[...] = wout_ref[columns, :].astype(F32).T.astype(BF16)
    noisep[...] = pack(noise_ref[0])
    step_coef = sizes_ref[tau]
    noise_coef = scales_ref[tau]

    u[240:256, :] = jnp.zeros((16, u.shape[1]), BF16)
    vt[:, 64:80, :] = jnp.ones((2, 16, vt.shape[2]), BF16)
    qt[...] = jnp.zeros_like(qt)

    exchange.wait_send()
    pltpu.make_async_remote_copy(
        src_ref=mw.at[other], dst_ref=mw.at[other], send_sem=msend, recv_sem=mrecv,
        device_id=partner, device_id_type=MESH,
    ).wait_recv()
    gather_finish(gb0, 0)
    assemble(gb0, True)

    def project(chunk, own):
        lanes = slice(chunk * BLOCK, chunk * BLOCK + BLOCK)
        part = u[:, lanes]
        mixed = dot(gw[...], part)
        square = jnp.sum(mixed * part[0:64].astype(F32), axis=0, keepdims=True)
        flags = part[192:208].astype(F32)
        square = square + jnp.sum(flags * ncol[:, 0:1], axis=0, keepdims=True)
        scale = lax.rsqrt(jnp.maximum(square, 0.0) * (1.0 / 2048) + 1e-06)
        keys = dot(jnp.concatenate([mw[0, 64:128], mw[1, 64:128]], axis=0), part) * scale
        k2[lanes, :] = keys.T.astype(BF16)
        values = dot(jnp.concatenate([mw[0, 128:192], mw[1, 128:192]], axis=0), part) * scale
        vt[0, 0:64, lanes] = values[0:64].astype(BF16)
        vt[1, 0:64, lanes] = values[64:128].astype(BF16)
        if own:
            queries = dot(jnp.concatenate([mw[0, 0:64], mw[1, 0:64]], axis=0), part)
            queries = queries * (scale * (0.125 * math.log2(math.e)))
            qt[0, 0:64, lanes] = queries[0:64].astype(BF16)
            qt[1, 64:128, lanes] = queries[64:128].astype(BF16)
            ht[:, lanes] = dot(hw[...], part)

    def partial_copy(sweep, slot):
        return pltpu.make_async_remote_copy(
            src_ref=pout.at[slot],
            dst_ref=pin.at[sweep, slot],
            send_sem=psend.at[slot],
            recv_sem=precv.at[sweep, slot],
            device_id=along(slot_offset(slot)),
            device_id_type=MESH,
        )

    def scores(index, into):
        block, head = index // 2, index % 2
        into[...] = dot(k2[...], qt[head, :, block * BLOCK : block * BLOCK + BLOCK])

    def attend(index, held):
        head = index % 2
        score = held[...]
        peak = jnp.max(score, axis=0, keepdims=True)
        probs = jnp.exp2(score - peak).astype(BF16)
        result = dot(vt[head], probs)
        return (result[0:64] * (1.0 / result[64:65])).astype(BF16)

    def hand_out(sweep, block, first, second):
        mixed = ht[:, block * BLOCK : block * BLOCK + BLOCK]
        mixed = mixed + jnp.concatenate([first, second], axis=0).astype(F32)
        square = jnp.sum(mixed * mixed, axis=0, keepdims=True)
        gain_column = fgt[:, 0:1]
        share = dot(wot[...], (mixed * gain_column).astype(BF16))
        sq_high = square.astype(BF16).astype(F32)
        tail = jnp.concatenate(
            [sq_high, square - sq_high, jnp.zeros((14, BLOCK), F32)], axis=0
        )
        top = jnp.concatenate([share[0:HALF], tail], axis=0)
        bottom = jnp.concatenate([share[HALF:64], tail], axis=0)
        for pair in range(BLOCK // 128):
            a = top[:, pair * 128 : pair * 128 + 128]
            b = bottom[:, pair * 128 : pair * 128 + 128]
            slot = block * 8 + 2 * pair
            left = jnp.concatenate([a[:, :64], b[:, :64]], axis=1).astype(BF16)
            right = jnp.concatenate([a[:, 64:], b[:, 64:]], axis=1).astype(BF16)
            pout[slot] = left
            partial_copy(sweep, slot).start()
            if slot + 1 < 15:
                pout[slot + 1] = right
                partial_copy(sweep, slot + 1).start()
            else:
                pin[sweep, 15] = right

    def one_sweep(sweep, carry):
        for chunk in range(4):
            project(chunk, chunk < 2)
        scores(0, s0)
        scores(1, s1)
        first = attend(0, s0)
        scores(2, s0)
        second = attend(1, s1)
        hand_out(sweep, 0, first, second)
        scores(3, s1)
        first = attend(2, s0)
        second = attend(3, s1)
        hand_out(sweep, 1, first, second)

        def landed(slot, carry):
            pltpu.make_async_remote_copy(
                src_ref=pout.at[slot], dst_ref=pin.at[sweep, slot],
                send_sem=psend.at[slot], recv_sem=precv.at[sweep, slot],
                device_id=partner, device_id_type=MESH,
            ).wait()
            return carry

        lax.fori_loop(0, 15, landed, 0)
        total = jnp.sum(pin[sweep].astype(F32), axis=0)
        square = total[HALF : HALF + 1] + total[HALF + 1 : HALF + 2]
        scale = lax.rsqrt(square * (1.0 / 2048) + 1e-06)
        own = step_coef * (total[0:HALF] * scale) + noise_coef * noisep[...]
        term[...] = own

        def send_term(later, carry):
            pltpu.make_async_remote_copy(
                src_ref=term, dst_ref=prefix.at[sweep, tm],
                send_sem=tsend.at[later], recv_sem=trecv.at[sweep, tm],
                device_id=(later, sq), device_id_type=MESH,
            ).start()
            return carry

        lax.fori_loop(tm + 1, STEPS, send_term, 0)

        def add_term(earlier, acc):
            pltpu.make_async_remote_copy(
                src_ref=term, dst_ref=prefix.at[sweep, earlier],
                send_sem=tsend.at[earlier], recv_sem=trecv.at[sweep, earlier],
                device_id=(earlier, sq), device_id_type=MESH,
            ).wait_recv()
            return acc + prefix[sweep, earlier]

        before = lax.fori_loop(0, tm, add_term, lsp[...])

        @pl.when(sweep == 0)
        def _():
            gb1[c, 15] = before.astype(BF16)
            gather_start(gb1, 1)
            gather_finish(gb1, 1)
            assemble(gb1, False)

        @pl.when(sweep == 1)
        def _():
            last = before + own
            out_ref[0] = jnp.concatenate([last[:, :64], last[:, 64:]], axis=0).T

        def sent_term(later, carry):
            pltpu.make_async_remote_copy(
                src_ref=term, dst_ref=prefix.at[sweep, tm],
                send_sem=tsend.at[later], recv_sem=trecv.at[sweep, tm],
                device_id=(later, sq), device_id_type=MESH,
            ).wait_send()
            return carry

        lax.fori_loop(tm + 1, STEPS, sent_term, 0)
        return carry

    lax.fori_loop(0, 2, one_sweep, 0)


def body(
    latent_start, noise, step_index, camera_ids, embed_in, time_table, camera_table, norm_gain,
    qkv_weight, final_gain, out_weight, step_sizes, noise_scales,
):
    vmem = pl.BlockSpec(memory_space=pltpu.VMEM)
    smem = pl.BlockSpec(memory_space=pltpu.SMEM)
    tokens = TOK * 2 * CHIPS
    dma = pltpu.SemaphoreType.DMA
    return pl.pallas_call(
        kernel,
        out_shape=jax.ShapeDtypeStruct((1, TOK, 64), F32),
        in_specs=[vmem, vmem, smem] + [vmem] * 8 + [smem, smem],
        out_specs=vmem,
        scratch_shapes=[
            pltpu.VMEM((HALF, 128), F32),
            pltpu.VMEM((HALF, 128), F32),
            pltpu.VMEM((2, 16, 48, 128), BF16),
            pltpu.VMEM((2, 16, HALF, 128), BF16),
            pltpu.VMEM((256, tokens), BF16),
            pltpu.VMEM((2, 192, 256), BF16),
            pltpu.VMEM((128, 256), BF16),
            pltpu.VMEM((64, 256), BF16),
            pltpu.VMEM((16, 2048), F32),
            pltpu.VMEM((16, 128), F32),
            pltpu.VMEM((64, 128), BF16),
            pltpu.VMEM((128, 128), F32),
            pltpu.VMEM((tokens, 128), BF16),
            pltpu.VMEM((2, 80, tokens), BF16),
            pltpu.VMEM((2, 128, tokens // 2), BF16),
            pltpu.VMEM((128, tokens // 2), F32),
            pltpu.VMEM((tokens, BLOCK), F32),
            pltpu.VMEM((tokens, BLOCK), F32),
            pltpu.VMEM((16, 48, 128), BF16),
            pltpu.VMEM((2, 16, 48, 128), BF16),
            pltpu.VMEM((HALF, 128), F32),
            pltpu.VMEM((2, STEPS, HALF, 128), F32),
            dma((2, 16)), dma((2, 16)),
            dma((2, 3)), dma((2, 3)),
            dma, dma,
            dma((16,)), dma((2, 16)),
            dma((16,)), dma((2, 16)),
        ],
        compiler_params=pltpu.CompilerParams(
            collective_id=0, has_side_effects=True, vmem_limit_bytes=56 * 1024 * 1024
        ),
    )(
        latent_start, noise, step_index, camera_ids.reshape(1, TOK), embed_in, time_table,
        camera_table, norm_gain.reshape(1, -1), qkv_weight.reshape(qkv_weight.shape[0], -1),
        final_gain.reshape(1, -1), out_weight, step_sizes, noise_scales,
    )


def solution(mesh):
    in_specs = (
        P("seq", None), P("tm", "seq", None), P("tm"), P("seq"), P(), P(), P(), P(),
        P(None, "seq", None), P(), P(), P(), P(),
    )
    return jax.shard_map(
        body, mesh=mesh, in_specs=in_specs, out_specs=P("tm", "seq", None), check_vma=False
    )
```

```python
import functools
import math

import jax
import jax.numpy as jnp
from jax import lax
from jax.experimental import pallas as pl
from jax.experimental.pallas import tpu as pltpu
from jax.sharding import PartitionSpec as P

MESH = pl.DeviceIdType.MESH
F32 = jnp.float32
BF16 = jnp.bfloat16
TOK = 64
HALF = 32
CHIPS = 16
STEPS = 16
BLOCK = 256
RELAYS = ((9, 16), (3, 9), (0, 3))


def slot_offset(slot):
    half = slot // 2
    return 8 + half - (slot % 2) * (1 + 2 * half)


def mirror(slot):
    return 0 if slot == 0 else 15 if slot == 15 else slot + 1 if slot % 2 else slot - 1


def dot(a, b):
    return jnp.dot(a, b, preferred_element_type=F32)


def dot_nt(a, b):
    return lax.dot_general(a, b, (((1,), (1,)), ((), ())), preferred_element_type=F32)


def split2(value):
    high = value.astype(BF16)
    return high, (value - high.astype(F32)).astype(BF16)


def split3(value):
    high = value.astype(BF16)
    rest = value - high.astype(F32)
    middle = rest.astype(BF16)
    return high, middle, (rest - middle.astype(F32)).astype(BF16)


def pack(block):
    flipped = block.T
    return jnp.concatenate([flipped[:HALF], flipped[HALF:]], axis=1)


def kernel(
    ls_ref, noise_hbm, step_ref, cam_ref, embed_hbm, time_hbm, camt_hbm, ngain_hbm, w_hbm,
    fgain_hbm, wout_hbm, sizes_ref, scales_ref,
    out_ref,
    noise_ref, embed_ref, time_ref, camt_ref, ngain_ref, w_ref, fgain_ref, loaded,
    lsp, noisep, gb, cams, u, mw, hw, gw, table, ncol, wot, fgt, k2, vt, qt, ht, s0, s1,
    pout, pin, qout, qin, term, prefix,
    gsend, grecv, rsend, rrecv, csend, crecv, ksend, krecv, msend, mrecv,
    psend, precv, qsend, qrecv, tsend, trecv,
):
    tm, sq = lax.axis_index("tm"), lax.axis_index("seq")
    z, c = sq // 2, sq % 2
    other = 1 - c
    partner = (tm, 2 * z + other)

    def along(offset):
        return (tm, 2 * ((z + offset) % CHIPS) + c)

    barrier = pltpu.get_barrier_semaphore()

    def greet_z(i, carry):
        pl.semaphore_signal(barrier, inc=1, device_id=along(i), device_id_type=MESH)
        return carry

    def greet_tm(i, carry):
        pl.semaphore_signal(
            barrier, inc=1, device_id=((tm + i) % STEPS, sq), device_id_type=MESH
        )
        return carry

    lax.fori_loop(1, CHIPS, greet_z, 0)
    lax.fori_loop(1, STEPS, greet_tm, 0)
    pl.semaphore_signal(barrier, inc=1, device_id=partner, device_id_type=MESH)

    columns = pl.ds(pl.multiple_of(z * 128, 128), 128)
    loads = [
        pltpu.make_async_copy(source, target, loaded.at[index])
        for index, (source, target) in enumerate(
            (
                (time_hbm, time_ref), (camt_hbm, camt_ref), (embed_hbm, embed_ref),
                (ngain_hbm, ngain_ref), (w_hbm, w_ref), (noise_hbm, noise_ref),
                (fgain_hbm.at[:, columns], fgain_ref), (wout_hbm.at[:, columns], wot),
            )
        )
    ]
    for load in loads:
        load.start()

    lsp[...] = pack(ls_ref[...])
    gb[0, c, 15] = lsp[...].astype(BF16)
    cam = cam_ref[...].astype(F32)
    cams[c, 15] = jnp.concatenate([cam, cam], axis=1)

    pl.semaphore_wait(barrier, CHIPS - 1 + STEPS - 1 + 1)

    def gather_copy(buf, send, recv, slot, into):
        return pltpu.make_async_remote_copy(
            src_ref=buf.at[c, 15],
            dst_ref=buf.at[c, into],
            send_sem=send.at[slot],
            recv_sem=recv.at[into],
            device_id=along(slot_offset(slot)),
            device_id_type=MESH,
        )

    def relay_copy(buf, send, recv, index, core):
        first, last = RELAYS[index]
        part = buf.at[core, pl.ds(first, last - first)]
        return pltpu.make_async_remote_copy(
            src_ref=part,
            dst_ref=part,
            send_sem=send.at[index],
            recv_sem=recv.at[index],
            device_id=partner,
            device_id_type=MESH,
        )

    latents = [
        (gb.at[phase], gsend.at[phase], grecv.at[phase], rsend.at[phase], rrecv.at[phase])
        for phase in range(2)
    ]
    cameras = (cams, csend, crecv, ksend, krecv)

    def gather_start(*arrays):
        for slot in range(15):
            for buf, send, recv, _, _ in arrays:
                gather_copy(buf, send, recv, slot, mirror(slot)).start()

    def gather_finish(*arrays):
        for index, (first, last) in enumerate(RELAYS):
            for buf, send, recv, again, landing in arrays:
                for slot in reversed(range(first, min(last, 15))):
                    gather_copy(buf, send, recv, slot, slot).wait_recv()
                relay_copy(buf, again, landing, index, c).start()
        for index in range(len(RELAYS)):
            for buf, _, _, again, landing in arrays:
                relay_copy(buf, again, landing, index, other).wait_recv()
        for buf, send, recv, again, landing in arrays:
            for slot in range(15):
                gather_copy(buf, send, recv, slot, mirror(slot)).wait_send()
            for index in range(len(RELAYS)):
                relay_copy(buf, again, landing, index, c).wait_send()

    def assemble(phase):
        for side in range(2):
            core = c if side == 0 else other
            for pair in range(8):
                lanes = slice(side * 1024 + pair * 128, side * 1024 + pair * 128 + 128)
                left = gb[phase, core, 2 * pair]
                right = gb[phase, core, 2 * pair + 1]
                low = jnp.concatenate([left[:, :64], right[:, :64]], axis=1)
                high = jnp.concatenate([left[:, 64:], right[:, 64:]], axis=1)
                tile = jnp.concatenate([low, high], axis=0)
                u[0:64, lanes] = tile
                u[64:128, lanes] = tile
                u[128:192, lanes] = tile
                if phase == 0:
                    near = lax.broadcasted_iota(jnp.int32, (1, 128), 1) < 64
                    ids = jnp.where(near, cams[core, 2 * pair], cams[core, 2 * pair + 1])
                    row = lax.broadcasted_iota(jnp.int32, (16, 128), 0).astype(F32)
                    one = jnp.where(ids == row, 1.0, 0.0).astype(BF16)
                    u[192:208, lanes] = one
                    u[208:224, lanes] = one
                    u[224:240, lanes] = one

    gather_start(latents[0], cameras)
    for load in loads:
        load.wait()

    tau = step_ref[0]
    rows = camt_ref[...] + time_ref[pl.ds(tau, 1), :]
    rows = jnp.concatenate([rows, jnp.zeros((10, rows.shape[1]), F32)], axis=0)
    table[...] = rows
    embed = embed_ref[...]
    gain = ngain_ref[...]
    eg_high, eg_low = split2(embed.astype(F32) * gain)
    rg_high, rg_low = split2(rows * gain)
    folded = dot_nt(jnp.concatenate([eg_high, rg_high, eg_low, rg_low], axis=0), w_ref[...])
    fold_x = folded[0:64] + folded[80:144]
    fold_e = folded[64:80] + folded[144:160]
    fx_high = fold_x.astype(BF16).astype(F32)
    fe_high = fold_e.astype(BF16).astype(F32)
    width = fold_x.shape[1]
    stacked = jnp.concatenate(
        [
            fx_high, fold_x - fx_high, jnp.zeros((64, width), F32),
            fe_high, fold_e - fe_high, jnp.zeros((32, width), F32),
        ],
        axis=0,
    )
    mw[c] = stacked.T.astype(BF16)
    exchange = pltpu.make_async_remote_copy(
        src_ref=mw.at[c], dst_ref=mw.at[c], send_sem=msend, recv_sem=mrecv,
        device_id=partner, device_id_type=MESH,
    )
    exchange.start()

    gram = dot_nt(embed, embed)
    r_high, r_middle, r_low = split3(rows)
    cross = 2.0 * (dot_nt(r_low, embed) + dot_nt(r_middle, embed) + dot_nt(r_high, embed))
    g3 = [part.astype(F32) for part in split3(gram)]
    c3 = [part.astype(F32) for part in split3(cross)]
    gw[...] = jnp.concatenate(g3 + c3 + [jnp.zeros((16, 64), F32)], axis=0).T.astype(BF16)
    ncol[...] = jnp.broadcast_to(jnp.sum(rows * rows, axis=1, keepdims=True), ncol.shape)

    h3 = [part.astype(F32) for part in split3(table[:, columns])]
    hw[...] = jnp.concatenate(
        [embed_ref[:, columns].astype(F32), jnp.zeros((128, 128), F32)]
        + h3
        + [jnp.zeros((16, 128), F32)],
        axis=0,
    ).T.astype(BF16)
    fgt[...] = jnp.broadcast_to(fgain_ref[...], (128, 128)).T
    noisep[...] = pack(noise_ref[0])
    step_coef = sizes_ref[tau]
    noise_coef = scales_ref[tau]

    u[240:256, :] = jnp.zeros((16, u.shape[1]), BF16)
    vt[:, 64:80, :] = jnp.ones((2, 16, vt.shape[2]), BF16)
    qt[...] = jnp.zeros_like(qt)

    exchange.wait_send()
    pltpu.make_async_remote_copy(
        src_ref=mw.at[other], dst_ref=mw.at[other], send_sem=msend, recv_sem=mrecv,
        device_id=partner, device_id_type=MESH,
    ).wait_recv()
    gather_finish(latents[0], cameras)
    assemble(0)

    def project(chunk, own):
        lanes = slice(chunk * 512, chunk * 512 + 512)
        part = u[:, lanes]
        mixed = dot(gw[...], part)
        square = jnp.sum(mixed * part[0:64].astype(F32), axis=0, keepdims=True)
        flags = part[192:208].astype(F32)
        square = square + jnp.sum(flags * ncol[:, 0:1], axis=0, keepdims=True)
        scale = lax.rsqrt(jnp.maximum(square, 0.0) * (1.0 / 2048) + 1e-06)
        keys = dot(jnp.concatenate([mw[0, 64:128], mw[1, 64:128]], axis=0), part) * scale
        k2[lanes, :] = keys.T.astype(BF16)
        values = dot(jnp.concatenate([mw[0, 128:192], mw[1, 128:192]], axis=0), part) * scale
        vt[0, 0:64, lanes] = values[0:64].astype(BF16)
        vt[1, 0:64, lanes] = values[64:128].astype(BF16)
        if own:
            queries = dot(jnp.concatenate([mw[0, 0:64], mw[1, 0:64]], axis=0), part)
            queries = queries * (scale * (0.125 * math.log2(math.e)))
            qt[0, 0:64, lanes] = queries[0:64].astype(BF16)
            qt[1, 64:128, lanes] = queries[64:128].astype(BF16)
            ht[:, lanes] = dot(hw[...], part)

    def partial_copies(sweep, slot):
        return [
            pltpu.make_async_remote_copy(
                src_ref=source.at[slot],
                dst_ref=target.at[sweep, slot],
                send_sem=send.at[slot],
                recv_sem=recv.at[sweep, slot],
                device_id=along(slot_offset(slot)),
                device_id_type=MESH,
            )
            for source, target, send, recv in (
                (pout, pin, psend, precv), (qout, qin, qsend, qrecv)
            )
        ]

    def scores(index, into):
        block, head = index // 2, index % 2
        into[...] = dot(k2[...], qt[head, :, block * BLOCK : block * BLOCK + BLOCK])

    def attend(index, held):
        head = index % 2
        score = held[...]
        peak = jnp.max(score, axis=0, keepdims=True)
        probs = jnp.exp2(score - peak).astype(BF16)
        result = dot(vt[head], probs)
        return (result[0:64] * (1.0 / result[64:65])).astype(BF16)

    def hand_out(sweep, block, first, second):
        mixed = ht[:, block * BLOCK : block * BLOCK + BLOCK]
        mixed = mixed + jnp.concatenate([first, second], axis=0).astype(F32)
        square = jnp.sum(mixed * mixed, axis=0, keepdims=True)
        high, low = split2(mixed * fgt[:, 0:1])
        weight = wot[...]
        share = dot(
            jnp.concatenate([weight, weight], axis=1), jnp.concatenate([high, low], axis=0)
        )
        for pair in range(BLOCK // 128):
            lanes = slice(pair * 128, pair * 128 + 128)
            a, b, s = share[0:HALF, lanes], share[HALF:64, lanes], square[:, lanes]
            for side in range(2):
                slot = block * (BLOCK // TOK) + 2 * pair + side
                half = slice(64 * side, 64 * side + 64)
                packed = jnp.concatenate([a[:, half], b[:, half]], axis=1).astype(BF16)
                squares = jnp.concatenate([s[:, half], s[:, half]], axis=1)
                if slot < 15:
                    pout[slot] = packed
                    qout[slot] = squares
                    for copy in partial_copies(sweep, slot):
                        copy.start()
                else:
                    pin[sweep, 15] = packed
                    qin[sweep, 15] = squares

    def one_sweep(sweep, carry):
        for chunk in range(4):
            project(chunk, chunk < 2)
        held = (s0, s1)
        steps = 2 * (1024 // BLOCK)
        scores(0, s0)
        results = []
        for index in range(steps):
            if index + 1 < steps:
                scores(index + 1, held[(index + 1) % 2])
            results.append(attend(index, held[index % 2]))
            if index % 2:
                hand_out(sweep, index // 2, results[index - 1], results[index])

        def landed(slot, carry):
            for copy in partial_copies(sweep, slot):
                copy.wait()
            return carry

        lax.fori_loop(0, 15, landed, 0)
        total = jnp.sum(pin[sweep].astype(F32), axis=0)
        square = jnp.sum(qin[sweep], axis=0)
        scale = lax.rsqrt(square * (1.0 / 2048) + 1e-06)
        own = step_coef * (total * scale) + noise_coef * noisep[...]
        term[...] = own

        def send_term(later, carry):
            pltpu.make_async_remote_copy(
                src_ref=term, dst_ref=prefix.at[sweep, tm],
                send_sem=tsend.at[later], recv_sem=trecv.at[sweep, tm],
                device_id=(later, sq), device_id_type=MESH,
            ).start()
            return carry

        lax.fori_loop(tm + 1, STEPS, send_term, 0)

        def add_term(earlier, acc):
            pltpu.make_async_remote_copy(
                src_ref=term, dst_ref=prefix.at[sweep, earlier],
                send_sem=tsend.at[earlier], recv_sem=trecv.at[sweep, earlier],
                device_id=(earlier, sq), device_id_type=MESH,
            ).wait_recv()
            return acc + prefix[sweep, earlier]

        before = lax.fori_loop(0, tm, add_term, lsp[...])

        @pl.when(sweep == 0)
        def _():
            gb[1, c, 15] = before.astype(BF16)
            gather_start(latents[1])
            gather_finish(latents[1])
            assemble(1)

        @pl.when(sweep == 1)
        def _():
            last = before + own
            out_ref[0] = jnp.concatenate([last[:, :64], last[:, 64:]], axis=0).T

        def sent_term(later, carry):
            pltpu.make_async_remote_copy(
                src_ref=term, dst_ref=prefix.at[sweep, tm],
                send_sem=tsend.at[later], recv_sem=trecv.at[sweep, tm],
                device_id=(later, sq), device_id_type=MESH,
            ).wait_send()
            return carry

        lax.fori_loop(tm + 1, STEPS, sent_term, 0)
        return carry

    lax.fori_loop(0, 2, one_sweep, 0)


def body(
    latent_start, noise, step_index, camera_ids, embed_in, time_table, camera_table, norm_gain,
    qkv_weight, final_gain, out_weight, step_sizes, noise_scales,
):
    vmem = pl.BlockSpec(memory_space=pltpu.VMEM)
    smem = pl.BlockSpec(memory_space=pltpu.SMEM)
    hbm = pl.BlockSpec(memory_space=pl.ANY)
    tokens = TOK * 2 * CHIPS
    dma = pltpu.SemaphoreType.DMA
    return pl.pallas_call(
        kernel,
        out_shape=jax.ShapeDtypeStruct((1, TOK, 64), F32),
        in_specs=[vmem, hbm, smem, vmem] + [hbm] * 7 + [smem, smem],
        out_specs=vmem,
        scratch_shapes=[
            pltpu.VMEM((1, TOK, 64), F32),
            pltpu.VMEM((64, 2048), BF16),
            pltpu.VMEM((50, 2048), F32),
            pltpu.VMEM((6, 2048), F32),
            pltpu.VMEM((1, 2048), F32),
            pltpu.VMEM((192, 2048), BF16),
            pltpu.VMEM((1, 128), F32),
            dma((8,)),
            pltpu.VMEM((HALF, 128), F32),
            pltpu.VMEM((HALF, 128), F32),
            pltpu.VMEM((2, 2, 16, HALF, 128), BF16),
            pltpu.VMEM((2, 16, 1, 128), F32),
            pltpu.VMEM((256, tokens), BF16),
            pltpu.VMEM((2, 192, 256), BF16),
            pltpu.VMEM((128, 256), BF16),
            pltpu.VMEM((64, 256), BF16),
            pltpu.VMEM((16, 2048), F32),
            pltpu.VMEM((16, 128), F32),
            pltpu.VMEM((64, 128), BF16),
            pltpu.VMEM((128, 128), F32),
            pltpu.VMEM((tokens, 128), BF16),
            pltpu.VMEM((2, 80, tokens), BF16),
            pltpu.VMEM((2, 128, tokens // 2), BF16),
            pltpu.VMEM((128, tokens // 2), F32),
            pltpu.VMEM((tokens, BLOCK), F32),
            pltpu.VMEM((tokens, BLOCK), F32),
            pltpu.VMEM((16, HALF, 128), BF16),
            pltpu.VMEM((2, 16, HALF, 128), BF16),
            pltpu.VMEM((16, 1, 128), F32),
            pltpu.VMEM((2, 16, 1, 128), F32),
            pltpu.VMEM((HALF, 128), F32),
            pltpu.VMEM((2, STEPS, HALF, 128), F32),
            dma((2, 16)), dma((2, 16)),
            dma((2, 3)), dma((2, 3)),
            dma((16,)), dma((16,)),
            dma((3,)), dma((3,)),
            dma, dma,
            dma((16,)), dma((2, 16)),
            dma((16,)), dma((2, 16)),
            dma((16,)), dma((2, 16)),
        ],
        compiler_params=pltpu.CompilerParams(
            collective_id=0, has_side_effects=True, vmem_limit_bytes=56 * 1024 * 1024
        ),
    )(
        latent_start, noise, step_index, camera_ids.reshape(1, TOK), embed_in, time_table,
        camera_table, norm_gain.reshape(1, -1), jnp.transpose(qkv_weight, (1, 2, 0)).reshape(-1, qkv_weight.shape[0]),
        final_gain.reshape(1, -1), out_weight.T, step_sizes, noise_scales,
    )


def solution(mesh):
    in_specs = (
        P("seq", None), P("tm", "seq", None), P("tm"), P("seq"), P(), P(), P(), P(),
        P(None, "seq", None), P(), P(), P(), P(),
    )
    return jax.shard_map(
        body, mesh=mesh, in_specs=in_specs, out_specs=P("tm", "seq", None), check_vma=False
    )
```

```python
import functools
import math

import jax
import jax.numpy as jnp
from jax import lax
from jax.experimental import pallas as pl
from jax.experimental.pallas import tpu as pltpu
from jax.sharding import PartitionSpec as P

MESH = pl.DeviceIdType.MESH
F32 = jnp.float32
BF16 = jnp.bfloat16
TOK = 64
HALF = 32
CHIPS = 16
STEPS = 16
BLOCK = 256
RELAYS = ((9, 16), (3, 9), (0, 3))


def slot_offset(slot):
    half = slot // 2
    return 8 + half - (slot % 2) * (1 + 2 * half)


def mirror(slot):
    return 0 if slot == 0 else 15 if slot == 15 else slot + 1 if slot % 2 else slot - 1


def dot(a, b):
    return jnp.dot(a, b, preferred_element_type=F32)


def dot_nt(a, b):
    return lax.dot_general(a, b, (((1,), (1,)), ((), ())), preferred_element_type=F32)


def split2(value):
    high = value.astype(BF16)
    return high, (value - high.astype(F32)).astype(BF16)


def split3(value):
    high = value.astype(BF16)
    rest = value - high.astype(F32)
    middle = rest.astype(BF16)
    return high, middle, (rest - middle.astype(F32)).astype(BF16)


def pack(block):
    flipped = block.T
    return jnp.concatenate([flipped[:HALF], flipped[HALF:]], axis=1)


def kernel(
    ls_ref, noise_hbm, step_ref, cam_ref, embed_hbm, time_hbm, camt_hbm, ngain_hbm, w_hbm,
    fgain_hbm, wout_hbm, sizes_ref, scales_ref,
    out_ref,
    noise_ref, embed_ref, time_ref, camt_ref, ngain_ref, w_ref, fgain_ref, loaded,
    lsp, noisep, gb, cams, u, mw, hw, gw, table, ncol, wot, fgt, k2, vt, qt, ht, s0, s1,
    pout, pin, qout, qin, term, prefix,
    gsend, grecv, rsend, rrecv, csend, crecv, ksend, krecv, msend, mrecv,
    psend, precv, qsend, qrecv, tsend, trecv,
):
    tm, sq = lax.axis_index("tm"), lax.axis_index("seq")
    z, c = sq // 2, sq % 2
    other = 1 - c
    partner = (tm, 2 * z + other)

    def along(offset):
        return (tm, 2 * ((z + offset) % CHIPS) + c)

    barrier = pltpu.get_barrier_semaphore()

    def greet_z(i, carry):
        pl.semaphore_signal(barrier, inc=1, device_id=along(i), device_id_type=MESH)
        return carry

    def greet_tm(i, carry):
        pl.semaphore_signal(
            barrier, inc=1, device_id=((tm + i) % STEPS, sq), device_id_type=MESH
        )
        return carry

    lax.fori_loop(1, CHIPS, greet_z, 0)
    lax.fori_loop(1, STEPS, greet_tm, 0)
    pl.semaphore_signal(barrier, inc=1, device_id=partner, device_id_type=MESH)

    columns = pl.ds(pl.multiple_of(z * 128, 128), 128)
    loads = [
        pltpu.make_async_copy(source, target, loaded.at[index])
        for index, (source, target) in enumerate(
            (
                (time_hbm, time_ref), (camt_hbm, camt_ref), (embed_hbm, embed_ref),
                (ngain_hbm, ngain_ref), (w_hbm, w_ref), (noise_hbm, noise_ref),
                (fgain_hbm.at[:, columns], fgain_ref), (wout_hbm.at[:, columns], wot),
            )
        )
    ]
    for load in loads:
        load.start()

    lsp[...] = pack(ls_ref[...])
    gb[0, c, 15] = lsp[...].astype(BF16)
    cam = cam_ref[...].astype(F32)
    cams[c, 15] = jnp.concatenate([cam, cam], axis=1)

    pl.semaphore_wait(barrier, CHIPS - 1 + STEPS - 1 + 1)

    def gather_copy(buf, send, recv, slot, into):
        return pltpu.make_async_remote_copy(
            src_ref=buf.at[c, 15],
            dst_ref=buf.at[c, into],
            send_sem=send.at[slot],
            recv_sem=recv.at[into],
            device_id=along(slot_offset(slot)),
            device_id_type=MESH,
        )

    def relay_copy(buf, send, recv, index, core):
        first, last = RELAYS[index]
        part = buf.at[core, pl.ds(first, last - first)]
        return pltpu.make_async_remote_copy(
            src_ref=part,
            dst_ref=part,
            send_sem=send.at[index],
            recv_sem=recv.at[index],
            device_id=partner,
            device_id_type=MESH,
        )

    latents = [
        (gb.at[phase], gsend.at[phase], grecv.at[phase], rsend.at[phase], rrecv.at[phase])
        for phase in range(2)
    ]
    cameras = (cams, csend, crecv, ksend, krecv)

    def gather_start(*arrays):
        for slot in range(15):
            for buf, send, recv, _, _ in arrays:
                gather_copy(buf, send, recv, slot, mirror(slot)).start()

    def gather_finish(*arrays):
        for index, (first, last) in enumerate(RELAYS):
            for buf, send, recv, again, landing in arrays:
                for slot in reversed(range(first, min(last, 15))):
                    gather_copy(buf, send, recv, slot, slot).wait_recv()
                relay_copy(buf, again, landing, index, c).start()
        for index in range(len(RELAYS)):
            for buf, _, _, again, landing in arrays:
                relay_copy(buf, again, landing, index, other).wait_recv()

    def gather_sent(buf, send, recv, again, landing):
        for slot in range(15):
            gather_copy(buf, send, recv, slot, mirror(slot)).wait_send()
        for index in range(len(RELAYS)):
            relay_copy(buf, again, landing, index, c).wait_send()

    def assemble(phase):
        for side in range(2):
            core = c if side == 0 else other
            for pair in range(8):
                lanes = slice(side * 1024 + pair * 128, side * 1024 + pair * 128 + 128)
                left = gb[phase, core, 2 * pair]
                right = gb[phase, core, 2 * pair + 1]
                low = jnp.concatenate([left[:, :64], right[:, :64]], axis=1)
                high = jnp.concatenate([left[:, 64:], right[:, 64:]], axis=1)
                tile = jnp.concatenate([low, high], axis=0)
                u[0:64, lanes] = tile
                u[64:128, lanes] = tile
                u[128:192, lanes] = tile
                if phase == 0:
                    near = lax.broadcasted_iota(jnp.int32, (1, 128), 1) < 64
                    ids = jnp.where(near, cams[core, 2 * pair], cams[core, 2 * pair + 1])
                    row = lax.broadcasted_iota(jnp.int32, (16, 128), 0).astype(F32)
                    one = jnp.where(ids == row, 1.0, 0.0).astype(BF16)
                    u[192:208, lanes] = one
                    u[208:224, lanes] = one
                    u[224:240, lanes] = one

    gather_start(latents[0], cameras)
    for load in loads:
        load.wait()

    tau = step_ref[0]
    rows = camt_ref[...] + time_ref[pl.ds(tau, 1), :]
    rows = jnp.concatenate([rows, jnp.zeros((10, rows.shape[1]), F32)], axis=0)
    table[...] = rows
    embed = embed_ref[...]
    gain = ngain_ref[...]
    eg_high, eg_low = split2(embed.astype(F32) * gain)
    rg_high, rg_low = split2(rows * gain)
    folded = dot_nt(jnp.concatenate([eg_high, rg_high, eg_low, rg_low], axis=0), w_ref[...])
    fold_x = folded[0:64] + folded[80:144]
    fold_e = folded[64:80] + folded[144:160]
    fx_high = fold_x.astype(BF16).astype(F32)
    fe_high = fold_e.astype(BF16).astype(F32)
    width = fold_x.shape[1]
    stacked = jnp.concatenate(
        [
            fx_high, fold_x - fx_high, jnp.zeros((64, width), F32),
            fe_high, fold_e - fe_high, jnp.zeros((32, width), F32),
        ],
        axis=0,
    )
    mw[c] = stacked.T.astype(BF16)
    exchange = pltpu.make_async_remote_copy(
        src_ref=mw.at[c], dst_ref=mw.at[c], send_sem=msend, recv_sem=mrecv,
        device_id=partner, device_id_type=MESH,
    )
    exchange.start()

    gram = dot_nt(embed, embed)
    r_high, r_middle, r_low = split3(rows)
    cross = 2.0 * (dot_nt(r_low, embed) + dot_nt(r_middle, embed) + dot_nt(r_high, embed))
    g3 = [part.astype(F32) for part in split3(gram)]
    c3 = [part.astype(F32) for part in split3(cross)]
    gw[...] = jnp.concatenate(g3 + c3 + [jnp.zeros((16, 64), F32)], axis=0).T.astype(BF16)
    ncol[...] = jnp.broadcast_to(jnp.sum(rows * rows, axis=1, keepdims=True), ncol.shape)

    h3 = [part.astype(F32) for part in split3(table[:, columns])]
    hw[...] = jnp.concatenate(
        [embed_ref[:, columns].astype(F32), jnp.zeros((128, 128), F32)]
        + h3
        + [jnp.zeros((16, 128), F32)],
        axis=0,
    ).T.astype(BF16)
    fgt[...] = jnp.broadcast_to(fgain_ref[...], (128, 128)).T
    noisep[...] = pack(noise_ref[0])
    step_coef = sizes_ref[tau]
    noise_coef = scales_ref[tau]

    u[240:256, :] = jnp.zeros((16, u.shape[1]), BF16)
    vt[:, 64:80, :] = jnp.ones((2, 16, vt.shape[2]), BF16)
    qt[...] = jnp.zeros_like(qt)

    exchange.wait_send()
    pltpu.make_async_remote_copy(
        src_ref=mw.at[other], dst_ref=mw.at[other], send_sem=msend, recv_sem=mrecv,
        device_id=partner, device_id_type=MESH,
    ).wait_recv()
    gather_finish(latents[0], cameras)
    assemble(0)

    def project(chunk, own):
        lanes = slice(chunk * 512, chunk * 512 + 512)
        part = u[:, lanes]
        mixed = dot(gw[...], part)
        square = jnp.sum(mixed * part[0:64].astype(F32), axis=0, keepdims=True)
        flags = part[192:208].astype(F32)
        square = square + jnp.sum(flags * ncol[:, 0:1], axis=0, keepdims=True)
        scale = lax.rsqrt(jnp.maximum(square, 0.0) * (1.0 / 2048) + 1e-06)
        keys = dot(jnp.concatenate([mw[0, 64:128], mw[1, 64:128]], axis=0), part) * scale
        k2[lanes, :] = keys.T.astype(BF16)
        values = dot(jnp.concatenate([mw[0, 128:192], mw[1, 128:192]], axis=0), part) * scale
        vt[0, 0:64, lanes] = values[0:64].astype(BF16)
        vt[1, 0:64, lanes] = values[64:128].astype(BF16)
        if own:
            queries = dot(jnp.concatenate([mw[0, 0:64], mw[1, 0:64]], axis=0), part)
            queries = queries * (scale * (0.125 * math.log2(math.e)))
            qt[0, 0:64, lanes] = queries[0:64].astype(BF16)
            qt[1, 64:128, lanes] = queries[64:128].astype(BF16)
            ht[:, lanes] = dot(hw[...], part)

    def partial_copies(sweep, slot):
        return [
            pltpu.make_async_remote_copy(
                src_ref=source.at[slot],
                dst_ref=target.at[sweep, slot],
                send_sem=send.at[slot],
                recv_sem=recv.at[sweep, slot],
                device_id=along(slot_offset(slot)),
                device_id_type=MESH,
            )
            for source, target, send, recv in (
                (pout, pin, psend, precv), (qout, qin, qsend, qrecv)
            )
        ]

    def scores(index, into):
        block, head = index // 2, index % 2
        into[...] = dot(k2[...], qt[head, :, block * BLOCK : block * BLOCK + BLOCK])

    def attend(index, held):
        head = index % 2
        score = held[...]
        peak = jnp.max(score, axis=0, keepdims=True)
        probs = jnp.exp2(score - peak).astype(BF16)
        result = dot(vt[head], probs)
        return (result[0:64] * (1.0 / result[64:65])).astype(BF16)

    def hand_out(sweep, block, first, second):
        mixed = ht[:, block * BLOCK : block * BLOCK + BLOCK]
        mixed = mixed + jnp.concatenate([first, second], axis=0).astype(F32)
        square = jnp.sum(mixed * mixed, axis=0, keepdims=True)
        high, low = split2(mixed * fgt[:, 0:1])
        weight = wot[...]
        share = dot(
            jnp.concatenate([weight, weight], axis=1), jnp.concatenate([high, low], axis=0)
        )
        for pair in range(BLOCK // 128):
            lanes = slice(pair * 128, pair * 128 + 128)
            a, b, s = share[0:HALF, lanes], share[HALF:64, lanes], square[:, lanes]
            for side in range(2):
                slot = block * (BLOCK // TOK) + 2 * pair + side
                half = slice(64 * side, 64 * side + 64)
                packed = jnp.concatenate([a[:, half], b[:, half]], axis=1).astype(BF16)
                squares = jnp.concatenate([s[:, half], s[:, half]], axis=1)
                if slot < 15:
                    pout[slot] = packed
                    qout[slot] = squares
                    for copy in partial_copies(sweep, slot):
                        copy.start()
                else:
                    pin[sweep, 15] = packed
                    qin[sweep, 15] = squares

    def one_sweep(sweep, carry):
        for chunk in range(4):
            project(chunk, chunk < 2)
        held = (s0, s1)
        steps = 2 * (1024 // BLOCK)
        scores(0, s0)
        results = []
        for index in range(steps):
            if index + 1 < steps:
                scores(index + 1, held[(index + 1) % 2])
            results.append(attend(index, held[index % 2]))
            if index % 2:
                hand_out(sweep, index // 2, results[index - 1], results[index])

        gather_sent(
            gb.at[sweep], gsend.at[sweep], grecv.at[sweep], rsend.at[sweep], rrecv.at[sweep]
        )

        @pl.when(sweep == 0)
        def _():
            gather_sent(*cameras)

        for slot in range(15):
            for copy in partial_copies(sweep, slot):
                copy.wait_recv()
        total = jnp.sum(pin[sweep].astype(F32), axis=0)
        square = jnp.sum(qin[sweep], axis=0)
        scale = lax.rsqrt(square * (1.0 / 2048) + 1e-06)
        own = step_coef * (total * scale) + noise_coef * noisep[...]
        term[...] = own

        def send_term(later, carry):
            pltpu.make_async_remote_copy(
                src_ref=term, dst_ref=prefix.at[sweep, tm],
                send_sem=tsend.at[later], recv_sem=trecv.at[sweep, tm],
                device_id=(later, sq), device_id_type=MESH,
            ).start()
            return carry

        lax.fori_loop(tm + 1, STEPS, send_term, 0)

        for slot in range(15):
            for copy in partial_copies(sweep, slot):
                copy.wait_send()

        def sent_term(later, carry):
            pltpu.make_async_remote_copy(
                src_ref=term, dst_ref=prefix.at[sweep, tm],
                send_sem=tsend.at[later], recv_sem=trecv.at[sweep, tm],
                device_id=(later, sq), device_id_type=MESH,
            ).wait_send()
            return carry

        def add_term(earlier, acc):
            pltpu.make_async_remote_copy(
                src_ref=term, dst_ref=prefix.at[sweep, earlier],
                send_sem=tsend.at[earlier], recv_sem=trecv.at[sweep, earlier],
                device_id=(earlier, sq), device_id_type=MESH,
            ).wait_recv()
            return acc + prefix[sweep, earlier]

        before = lax.fori_loop(0, tm, add_term, lsp[...])

        @pl.when(sweep == 0)
        def _():
            gb[1, c, 15] = before.astype(BF16)
            gather_start(latents[1])
            lax.fori_loop(tm + 1, STEPS, sent_term, 0)
            gather_finish(latents[1])
            assemble(1)

        @pl.when(sweep == 1)
        def _():
            last = before + own
            out_ref[0] = jnp.concatenate([last[:, :64], last[:, 64:]], axis=0).T
            lax.fori_loop(tm + 1, STEPS, sent_term, 0)

        return carry

    lax.fori_loop(0, 2, one_sweep, 0)


def body(
    latent_start, noise, step_index, camera_ids, embed_in, time_table, camera_table, norm_gain,
    qkv_weight, final_gain, out_weight, step_sizes, noise_scales,
):
    vmem = pl.BlockSpec(memory_space=pltpu.VMEM)
    smem = pl.BlockSpec(memory_space=pltpu.SMEM)
    hbm = pl.BlockSpec(memory_space=pl.ANY)
    tokens = TOK * 2 * CHIPS
    dma = pltpu.SemaphoreType.DMA
    return pl.pallas_call(
        kernel,
        out_shape=jax.ShapeDtypeStruct((1, TOK, 64), F32),
        in_specs=[vmem, hbm, smem, vmem] + [hbm] * 7 + [smem, smem],
        out_specs=vmem,
        scratch_shapes=[
            pltpu.VMEM((1, TOK, 64), F32),
            pltpu.VMEM((64, 2048), BF16),
            pltpu.VMEM((50, 2048), F32),
            pltpu.VMEM((6, 2048), F32),
            pltpu.VMEM((1, 2048), F32),
            pltpu.VMEM((192, 2048), BF16),
            pltpu.VMEM((1, 128), F32),
            dma((8,)),
            pltpu.VMEM((HALF, 128), F32),
            pltpu.VMEM((HALF, 128), F32),
            pltpu.VMEM((2, 2, 16, HALF, 128), BF16),
            pltpu.VMEM((2, 16, 1, 128), F32),
            pltpu.VMEM((256, tokens), BF16),
            pltpu.VMEM((2, 192, 256), BF16),
            pltpu.VMEM((128, 256), BF16),
            pltpu.VMEM((64, 256), BF16),
            pltpu.VMEM((16, 2048), F32),
            pltpu.VMEM((16, 128), F32),
            pltpu.VMEM((64, 128), BF16),
            pltpu.VMEM((128, 128), F32),
            pltpu.VMEM((tokens, 128), BF16),
            pltpu.VMEM((2, 80, tokens), BF16),
            pltpu.VMEM((2, 128, tokens // 2), BF16),
            pltpu.VMEM((128, tokens // 2), F32),
            pltpu.VMEM((tokens, BLOCK), F32),
            pltpu.VMEM((tokens, BLOCK), F32),
            pltpu.VMEM((16, HALF, 128), BF16),
            pltpu.VMEM((2, 16, HALF, 128), BF16),
            pltpu.VMEM((16, 1, 128), F32),
            pltpu.VMEM((2, 16, 1, 128), F32),
            pltpu.VMEM((HALF, 128), F32),
            pltpu.VMEM((2, STEPS, HALF, 128), F32),
            dma((2, 16)), dma((2, 16)),
            dma((2, 3)), dma((2, 3)),
            dma((16,)), dma((16,)),
            dma((3,)), dma((3,)),
            dma, dma,
            dma((16,)), dma((2, 16)),
            dma((16,)), dma((2, 16)),
            dma((16,)), dma((2, 16)),
        ],
        compiler_params=pltpu.CompilerParams(
            collective_id=0, has_side_effects=True, vmem_limit_bytes=56 * 1024 * 1024
        ),
    )(
        latent_start, noise, step_index, camera_ids.reshape(1, TOK), embed_in, time_table,
        camera_table, norm_gain.reshape(1, -1), jnp.transpose(qkv_weight, (1, 2, 0)).reshape(-1, qkv_weight.shape[0]),
        final_gain.reshape(1, -1), out_weight.T, step_sizes, noise_scales,
    )


def solution(mesh):
    in_specs = (
        P("seq", None), P("tm", "seq", None), P("tm"), P("seq"), P(), P(), P(), P(),
        P(None, "seq", None), P(), P(), P(), P(),
    )
    return jax.shard_map(
        body, mesh=mesh, in_specs=in_specs, out_specs=P("tm", "seq", None), check_vma=False
    )
```

```python
import functools
import math

import jax
import jax.numpy as jnp
from jax import lax
from jax.experimental import pallas as pl
from jax.experimental.pallas import tpu as pltpu
from jax.sharding import PartitionSpec as P

MESH = pl.DeviceIdType.MESH
F32 = jnp.float32
BF16 = jnp.bfloat16
TOK = 64
HALF = 32
CHIPS = 16
STEPS = 16
BLOCK = 256
RELAYS = ((9, 16), (3, 9), (0, 3))


def slot_offset(slot):
    half = slot // 2
    return 8 + half - (slot % 2) * (1 + 2 * half)


def mirror(slot):
    return 0 if slot == 0 else 15 if slot == 15 else slot + 1 if slot % 2 else slot - 1


def dot(a, b):
    return jnp.dot(a, b, preferred_element_type=F32)


def dot_nt(a, b):
    return lax.dot_general(a, b, (((1,), (1,)), ((), ())), preferred_element_type=F32)


def split2(value):
    high = value.astype(BF16)
    return high, (value - high.astype(F32)).astype(BF16)


def split3(value):
    high = value.astype(BF16)
    rest = value - high.astype(F32)
    middle = rest.astype(BF16)
    return high, middle, (rest - middle.astype(F32)).astype(BF16)


def pack(block):
    flipped = block.T
    return jnp.concatenate([flipped[:HALF], flipped[HALF:]], axis=1)


def kernel(
    ls_ref, noise_hbm, step_ref, cam_ref, embed_hbm, time_hbm, camt_hbm, ngain_hbm, w_hbm,
    fgain_hbm, wout_hbm, sizes_ref, scales_ref,
    out_ref,
    noise_ref, embed_ref, time_ref, camt_ref, ngain_ref, w_ref, fgain_ref, loaded,
    lsp, noisep, gb, cams, u, mw, hw, gw, table, ncol, wot, fgt, k2, vt, qt, ht, s0, s1,
    pout, pin, qout, qin, term, prefix,
    gsend, grecv, rsend, rrecv, csend, crecv, ksend, krecv, msend, mrecv,
    psend, precv, qsend, qrecv, tsend, trecv,
):
    tm, sq = lax.axis_index("tm"), lax.axis_index("seq")
    z, c = sq // 2, sq % 2
    other = 1 - c
    partner = (tm, 2 * z + other)

    def along(offset):
        return (tm, 2 * ((z + offset) % CHIPS) + c)

    barrier = pltpu.get_barrier_semaphore()

    def greet_z(i, carry):
        pl.semaphore_signal(barrier, inc=1, device_id=along(i), device_id_type=MESH)
        return carry

    def greet_tm(i, carry):
        pl.semaphore_signal(
            barrier, inc=1, device_id=((tm + i) % STEPS, sq), device_id_type=MESH
        )
        return carry

    lax.fori_loop(1, CHIPS, greet_z, 0)
    lax.fori_loop(1, STEPS, greet_tm, 0)
    pl.semaphore_signal(barrier, inc=1, device_id=partner, device_id_type=MESH)

    columns = pl.ds(pl.multiple_of(z * 128, 128), 128)
    loads = [
        pltpu.make_async_copy(source, target, loaded.at[index])
        for index, (source, target) in enumerate(
            (
                (time_hbm, time_ref), (camt_hbm, camt_ref), (embed_hbm, embed_ref),
                (ngain_hbm, ngain_ref), (w_hbm, w_ref), (noise_hbm, noise_ref),
                (fgain_hbm.at[:, columns], fgain_ref), (wout_hbm.at[:, columns], wot),
            )
        )
    ]
    for load in loads:
        load.start()

    lsp[...] = pack(ls_ref[...])
    gb[0, c, 15] = lsp[...].astype(BF16)
    cam = cam_ref[...].astype(F32)
    cams[c, 15] = jnp.concatenate([cam, cam], axis=1)

    pl.semaphore_wait(barrier, CHIPS - 1 + STEPS - 1 + 1)

    def gather_copy(buf, send, recv, slot, into):
        return pltpu.make_async_remote_copy(
            src_ref=buf.at[c, 15],
            dst_ref=buf.at[c, into],
            send_sem=send.at[slot],
            recv_sem=recv.at[into],
            device_id=along(slot_offset(slot)),
            device_id_type=MESH,
        )

    def relay_copy(buf, send, recv, index, core):
        first, last = RELAYS[index]
        part = buf.at[core, pl.ds(first, last - first)]
        return pltpu.make_async_remote_copy(
            src_ref=part,
            dst_ref=part,
            send_sem=send.at[index],
            recv_sem=recv.at[index],
            device_id=partner,
            device_id_type=MESH,
        )

    latents = [
        (gb.at[phase], gsend.at[phase], grecv.at[phase], rsend.at[phase], rrecv.at[phase])
        for phase in range(2)
    ]
    cameras = (cams, csend, crecv, ksend, krecv)

    def gather_start(*arrays):
        for slot in range(15):
            for buf, send, recv, _, _ in arrays:
                gather_copy(buf, send, recv, slot, mirror(slot)).start()

    def gather_finish(*arrays):
        for buf, send, recv, again, landing in arrays:
            for index, (first, last) in enumerate(RELAYS):
                for slot in reversed(range(first, min(last, 15))):
                    gather_copy(buf, send, recv, slot, slot).wait_recv()
                relay_copy(buf, again, landing, index, c).start()
        for index in range(len(RELAYS)):
            for buf, _, _, again, landing in arrays:
                relay_copy(buf, again, landing, index, other).wait_recv()

    def gather_sent(buf, send, recv, again, landing):
        for slot in range(15):
            gather_copy(buf, send, recv, slot, mirror(slot)).wait_send()
        for index in range(len(RELAYS)):
            relay_copy(buf, again, landing, index, c).wait_send()

    def assemble(phase):
        for side in range(2):
            core = c if side == 0 else other
            for pair in range(8):
                lanes = slice(side * 1024 + pair * 128, side * 1024 + pair * 128 + 128)
                left = gb[phase, core, 2 * pair]
                right = gb[phase, core, 2 * pair + 1]
                low = jnp.concatenate([left[:, :64], right[:, :64]], axis=1)
                high = jnp.concatenate([left[:, 64:], right[:, 64:]], axis=1)
                tile = jnp.concatenate([low, high], axis=0)
                u[0:64, lanes] = tile
                u[64:128, lanes] = tile
                u[128:192, lanes] = tile
                if phase == 0:
                    near = lax.broadcasted_iota(jnp.int32, (1, 128), 1) < 64
                    ids = jnp.where(near, cams[core, 2 * pair], cams[core, 2 * pair + 1])
                    row = lax.broadcasted_iota(jnp.int32, (16, 128), 0).astype(F32)
                    one = jnp.where(ids == row, 1.0, 0.0).astype(BF16)
                    u[192:208, lanes] = one
                    u[208:224, lanes] = one
                    u[224:240, lanes] = one

    gather_start(latents[0], cameras)
    for load in loads:
        load.wait()

    tau = step_ref[0]
    rows = camt_ref[...] + time_ref[pl.ds(tau, 1), :]
    rows = jnp.concatenate([rows, jnp.zeros((10, rows.shape[1]), F32)], axis=0)
    table[...] = rows
    embed = embed_ref[...]
    gain = ngain_ref[...]
    eg_high, eg_low = split2(embed.astype(F32) * gain)
    rg_high, rg_low = split2(rows * gain)
    folded = dot_nt(jnp.concatenate([eg_high, rg_high, eg_low, rg_low], axis=0), w_ref[...])
    fold_x = folded[0:64] + folded[80:144]
    fold_e = folded[64:80] + folded[144:160]
    fx_high = fold_x.astype(BF16).astype(F32)
    fe_high = fold_e.astype(BF16).astype(F32)
    width = fold_x.shape[1]
    stacked = jnp.concatenate(
        [
            fx_high, fold_x - fx_high, jnp.zeros((64, width), F32),
            fe_high, fold_e - fe_high, jnp.zeros((32, width), F32),
        ],
        axis=0,
    )
    mw[c] = stacked.T.astype(BF16)
    exchange = pltpu.make_async_remote_copy(
        src_ref=mw.at[c], dst_ref=mw.at[c], send_sem=msend, recv_sem=mrecv,
        device_id=partner, device_id_type=MESH,
    )
    exchange.start()

    gram = dot_nt(embed, embed)
    r_high, r_middle, r_low = split3(rows)
    cross = 2.0 * (dot_nt(r_low, embed) + dot_nt(r_middle, embed) + dot_nt(r_high, embed))
    g3 = [part.astype(F32) for part in split3(gram)]
    c3 = [part.astype(F32) for part in split3(cross)]
    gw[...] = jnp.concatenate(g3 + c3 + [jnp.zeros((16, 64), F32)], axis=0).T.astype(BF16)
    ncol[...] = jnp.broadcast_to(jnp.sum(rows * rows, axis=1, keepdims=True), ncol.shape)

    h3 = [part.astype(F32) for part in split3(table[:, columns])]
    hw[...] = jnp.concatenate(
        [embed_ref[:, columns].astype(F32), jnp.zeros((128, 128), F32)]
        + h3
        + [jnp.zeros((16, 128), F32)],
        axis=0,
    ).T.astype(BF16)
    fgt[...] = jnp.broadcast_to(fgain_ref[...], (128, 128)).T
    noisep[...] = pack(noise_ref[0])
    step_coef = sizes_ref[tau]
    noise_coef = scales_ref[tau]

    u[240:256, :] = jnp.zeros((16, u.shape[1]), BF16)
    vt[:, 64:80, :] = jnp.ones((2, 16, vt.shape[2]), BF16)
    qt[...] = jnp.zeros_like(qt)

    exchange.wait_send()
    pltpu.make_async_remote_copy(
        src_ref=mw.at[other], dst_ref=mw.at[other], send_sem=msend, recv_sem=mrecv,
        device_id=partner, device_id_type=MESH,
    ).wait_recv()
    gather_finish(latents[0], cameras)
    assemble(0)

    def project(chunk, own):
        lanes = slice(chunk * 512, chunk * 512 + 512)
        part = u[:, lanes]
        mixed = dot(gw[...], part)
        square = jnp.sum(mixed * part[0:64].astype(F32), axis=0, keepdims=True)
        flags = part[192:208].astype(F32)
        square = square + jnp.sum(flags * ncol[:, 0:1], axis=0, keepdims=True)
        scale = lax.rsqrt(jnp.maximum(square, 0.0) * (1.0 / 2048) + 1e-06)
        keys = dot(jnp.concatenate([mw[0, 64:128], mw[1, 64:128]], axis=0), part) * scale
        k2[lanes, :] = keys.T.astype(BF16)
        values = dot(jnp.concatenate([mw[0, 128:192], mw[1, 128:192]], axis=0), part) * scale
        vt[0, 0:64, lanes] = values[0:64].astype(BF16)
        vt[1, 0:64, lanes] = values[64:128].astype(BF16)
        if own:
            queries = dot(jnp.concatenate([mw[0, 0:64], mw[1, 0:64]], axis=0), part)
            queries = queries * (scale * (0.125 * math.log2(math.e)))
            qt[0, 0:64, lanes] = queries[0:64].astype(BF16)
            qt[1, 64:128, lanes] = queries[64:128].astype(BF16)
            ht[:, lanes] = dot(hw[...], part)

    def partial_copies(sweep, slot):
        return [
            pltpu.make_async_remote_copy(
                src_ref=source.at[slot],
                dst_ref=target.at[sweep, slot],
                send_sem=send.at[slot],
                recv_sem=recv.at[sweep, slot],
                device_id=along(slot_offset(slot)),
                device_id_type=MESH,
            )
            for source, target, send, recv in (
                (pout, pin, psend, precv), (qout, qin, qsend, qrecv)
            )
        ]

    def scores(index, into):
        block, head = index // 2, index % 2
        into[...] = dot(k2[...], qt[head, :, block * BLOCK : block * BLOCK + BLOCK])

    def attend(index, held):
        head = index % 2
        score = held[...]
        peak = jnp.max(score, axis=0, keepdims=True)
        probs = jnp.exp2(score - peak).astype(BF16)
        result = dot(vt[head], probs)
        return (result[0:64] * (1.0 / result[64:65])).astype(BF16)

    def hand_out(sweep, block, first, second):
        mixed = ht[:, block * BLOCK : block * BLOCK + BLOCK]
        mixed = mixed + jnp.concatenate([first, second], axis=0).astype(F32)
        square = jnp.sum(mixed * mixed, axis=0, keepdims=True)
        high, low = split2(mixed * fgt[:, 0:1])
        weight = wot[...]
        share = dot(
            jnp.concatenate([weight, weight], axis=1), jnp.concatenate([high, low], axis=0)
        )
        for pair in range(BLOCK // 128):
            lanes = slice(pair * 128, pair * 128 + 128)
            a, b, s = share[0:HALF, lanes], share[HALF:64, lanes], square[:, lanes]
            for side in range(2):
                slot = block * (BLOCK // TOK) + 2 * pair + side
                half = slice(64 * side, 64 * side + 64)
                packed = jnp.concatenate([a[:, half], b[:, half]], axis=1).astype(BF16)
                squares = jnp.concatenate([s[:, half], s[:, half]], axis=1)
                if slot < 15:
                    pout[slot] = packed
                    qout[slot] = squares
                    for copy in partial_copies(sweep, slot):
                        copy.start()
                else:
                    pin[sweep, 15] = packed
                    qin[sweep, 15] = squares

    def one_sweep(sweep, carry):
        for chunk in range(4):
            project(chunk, chunk < 2)
        held = (s0, s1)
        steps = 2 * (1024 // BLOCK)
        scores(0, s0)
        results = []
        for index in range(steps):
            if index + 1 < steps:
                scores(index + 1, held[(index + 1) % 2])
            results.append(attend(index, held[index % 2]))
            if index % 2:
                hand_out(sweep, index // 2, results[index - 1], results[index])

        gather_sent(
            gb.at[sweep], gsend.at[sweep], grecv.at[sweep], rsend.at[sweep], rrecv.at[sweep]
        )

        @pl.when(sweep == 0)
        def _():
            gather_sent(*cameras)

        for slot in range(15):
            for copy in partial_copies(sweep, slot):
                copy.wait_recv()
        total = jnp.sum(pin[sweep].astype(F32), axis=0)
        square = jnp.sum(qin[sweep], axis=0)
        scale = lax.rsqrt(square * (1.0 / 2048) + 1e-06)
        own = step_coef * (total * scale) + noise_coef * noisep[...]
        term[...] = own

        def send_term(later, carry):
            pltpu.make_async_remote_copy(
                src_ref=term, dst_ref=prefix.at[sweep, tm],
                send_sem=tsend.at[later], recv_sem=trecv.at[sweep, tm],
                device_id=(later, sq), device_id_type=MESH,
            ).start()
            return carry

        lax.fori_loop(tm + 1, STEPS, send_term, 0)

        for slot in range(15):
            for copy in partial_copies(sweep, slot):
                copy.wait_send()

        def sent_term(later, carry):
            pltpu.make_async_remote_copy(
                src_ref=term, dst_ref=prefix.at[sweep, tm],
                send_sem=tsend.at[later], recv_sem=trecv.at[sweep, tm],
                device_id=(later, sq), device_id_type=MESH,
            ).wait_send()
            return carry

        def add_term(earlier, acc):
            pltpu.make_async_remote_copy(
                src_ref=term, dst_ref=prefix.at[sweep, earlier],
                send_sem=tsend.at[earlier], recv_sem=trecv.at[sweep, earlier],
                device_id=(earlier, sq), device_id_type=MESH,
            ).wait_recv()
            return acc + prefix[sweep, earlier]

        before = lax.fori_loop(0, tm, add_term, lsp[...])

        @pl.when(sweep == 0)
        def _():
            gb[1, c, 15] = before.astype(BF16)
            gather_start(latents[1])
            lax.fori_loop(tm + 1, STEPS, sent_term, 0)
            gather_finish(latents[1])
            assemble(1)

        @pl.when(sweep == 1)
        def _():
            last = before + own
            out_ref[0] = jnp.concatenate([last[:, :64], last[:, 64:]], axis=0).T
            lax.fori_loop(tm + 1, STEPS, sent_term, 0)

        return carry

    lax.fori_loop(0, 2, one_sweep, 0)


def body(
    latent_start, noise, step_index, camera_ids, embed_in, time_table, camera_table, norm_gain,
    qkv_weight, final_gain, out_weight, step_sizes, noise_scales,
):
    vmem = pl.BlockSpec(memory_space=pltpu.VMEM)
    smem = pl.BlockSpec(memory_space=pltpu.SMEM)
    hbm = pl.BlockSpec(memory_space=pl.ANY)
    tokens = TOK * 2 * CHIPS
    dma = pltpu.SemaphoreType.DMA
    return pl.pallas_call(
        kernel,
        out_shape=jax.ShapeDtypeStruct((1, TOK, 64), F32),
        in_specs=[vmem, hbm, smem, vmem] + [hbm] * 7 + [smem, smem],
        out_specs=vmem,
        scratch_shapes=[
            pltpu.VMEM((1, TOK, 64), F32),
            pltpu.VMEM((64, 2048), BF16),
            pltpu.VMEM((50, 2048), F32),
            pltpu.VMEM((6, 2048), F32),
            pltpu.VMEM((1, 2048), F32),
            pltpu.VMEM((192, 2048), BF16),
            pltpu.VMEM((1, 128), F32),
            dma((8,)),
            pltpu.VMEM((HALF, 128), F32),
            pltpu.VMEM((HALF, 128), F32),
            pltpu.VMEM((2, 2, 16, HALF, 128), BF16),
            pltpu.VMEM((2, 16, 1, 128), F32),
            pltpu.VMEM((256, tokens), BF16),
            pltpu.VMEM((2, 192, 256), BF16),
            pltpu.VMEM((128, 256), BF16),
            pltpu.VMEM((64, 256), BF16),
            pltpu.VMEM((16, 2048), F32),
            pltpu.VMEM((16, 128), F32),
            pltpu.VMEM((64, 128), BF16),
            pltpu.VMEM((128, 128), F32),
            pltpu.VMEM((tokens, 128), BF16),
            pltpu.VMEM((2, 80, tokens), BF16),
            pltpu.VMEM((2, 128, tokens // 2), BF16),
            pltpu.VMEM((128, tokens // 2), F32),
            pltpu.VMEM((tokens, BLOCK), F32),
            pltpu.VMEM((tokens, BLOCK), F32),
            pltpu.VMEM((16, HALF, 128), BF16),
            pltpu.VMEM((2, 16, HALF, 128), BF16),
            pltpu.VMEM((16, 1, 128), F32),
            pltpu.VMEM((2, 16, 1, 128), F32),
            pltpu.VMEM((HALF, 128), F32),
            pltpu.VMEM((2, STEPS, HALF, 128), F32),
            dma((2, 16)), dma((2, 16)),
            dma((2, 3)), dma((2, 3)),
            dma((16,)), dma((16,)),
            dma((3,)), dma((3,)),
            dma, dma,
            dma((16,)), dma((2, 16)),
            dma((16,)), dma((2, 16)),
            dma((16,)), dma((2, 16)),
        ],
        compiler_params=pltpu.CompilerParams(
            collective_id=0, has_side_effects=True, vmem_limit_bytes=56 * 1024 * 1024
        ),
    )(
        latent_start, noise, step_index, camera_ids.reshape(1, TOK), embed_in, time_table,
        camera_table, norm_gain.reshape(1, -1), jnp.transpose(qkv_weight, (1, 2, 0)).reshape(-1, qkv_weight.shape[0]),
        final_gain.reshape(1, -1), out_weight.T, step_sizes, noise_scales,
    )


def solution(mesh):
    in_specs = (
        P("seq", None), P("tm", "seq", None), P("tm"), P("seq"), P(), P(), P(), P(),
        P(None, "seq", None), P(), P(), P(), P(),
    )
    return jax.shard_map(
        body, mesh=mesh, in_specs=in_specs, out_specs=P("tm", "seq", None), check_vma=False
    )
```
